1024 devices in a mesh: occ: 64 (over z, x), aux: 16 (over y, core).
Axes of the slice: x: 8, y: 8, z: 8, core: 2. Of those that a mesh axis runs over, the one named last changes fastest.
Arguments:
- ri_blocks: bfloat16 [64, 48, 16384], P('occ', None, 'aux'), may hold values from -0.29882812 to 0.29882812
- blk_occ: int32 [64], replicated, may hold values from 0 to 39
- blk_virt: int32 [64], replicated, may hold values from 0 to 255
- live_count: int32 [64], replicated, may hold values from 1 to 48
- aux_mask: int32 [64, 64], replicated, may hold values 0 or 1
- occ_energy: float32 [40], replicated, may hold values from -2 to -0.3
- virt_energy: float32 [12288], replicated, may hold values from 0.1 to 3
- frequency: float32 [1], replicated, may hold values from 0.2 to 2
Outputs:
- response: float32 [16384, 16384], P('occ', 'aux')
The draws below stay inside these ranges and needn't reach their ends.
All inputs are finite; a program needn't handle non-finite values.
Results may differ from the reference program's by a relative error of at most 0.0028.
Values may be sent and summed in bfloat16 or wider, within the bound.
A program may use at most 64 MiB of HBM per device.

```python
import math
import jax
import jax.numpy as jnp
from jax import lax

NAUX = 16384
NVIRT = 12288
NOCC = 40
VBLK = 48
AB = 256
NBLK = 64
NVB = 256
NAB = 64
PIECE = 16
N_OCC = 64
N_AUX = 16


def touch_ends(result, stream_key, low, top_value):
    index_at = [jax.random.randint(jax.random.fold_in(stream_key, axis), (), 0, length) for axis, length in enumerate(result.shape)]
    widest = result.shape.index(max(result.shape))
    beside = index_at[:widest] + [(index_at[widest] + 1) % result.shape[widest]] + index_at[widest + 1:]
    return result.at[tuple(index_at)].set(low).at[tuple(beside)].set(top_value)


def steps_of(rng, shape, cuts, least, largest):
    factor_of, own = 1.0, jax.random.fold_in(rng, 6)
    for position, shards_of in cuts:
        heights = jnp.exp(jax.random.uniform(jax.random.fold_in(own, position), (shards_of,), jnp.float32, least / len(cuts), largest / len(cuts)))
        factor_of = factor_of * jnp.repeat(heights, shape[position] // shards_of).reshape([-1 if axis == position else 1 for axis in range(len(shape))])
    return factor_of


def normal_values(key, extent, width, reach, cuts=(), held_as=jnp.bfloat16):
    gain = steps_of(key, extent, cuts, -0.22, 0.18) if cuts else 1.0
    entries = jax.random.normal(key, extent, jnp.float32) * width * gain
    return jnp.minimum(jnp.maximum(entries, -reach), reach).astype(held_as)


def setup_inputs(seed: int = 0) -> dict:
    streams_of = jax.random.split(jax.random.key(seed), 9)
    return {
        "ri_blocks": normal_values(streams_of[0], (NBLK, VBLK, NAUX), 0.05, 0.29882812, ((0, 64), (2, 16))),
        "blk_occ": touch_ends(jax.random.randint(streams_of[1], (NBLK,), 0, NOCC), jax.random.fold_in(streams_of[1], 1), 0, NOCC - 1).astype(jnp.int32),
        "blk_virt": touch_ends(jax.random.randint(streams_of[2], (NBLK,), 0, NVB), jax.random.fold_in(streams_of[2], 1), 0, NVB - 1).astype(jnp.int32),
        "live_count": touch_ends(jax.random.randint(streams_of[3], (NBLK,), 1, VBLK + 1), jax.random.fold_in(streams_of[3], 1), 1, VBLK).astype(jnp.int32),
        "aux_mask": touch_ends((jax.random.randint(streams_of[4], (NBLK, NAB), 0, 3) < 2).astype(jnp.int32), jax.random.fold_in(streams_of[4], 1), 0, 1),
        "occ_energy": jnp.clip(jax.random.uniform(streams_of[5], (NOCC,), jnp.float32, -2.0, -0.3), -2.0, -0.3),
        "virt_energy": jnp.clip(jax.random.uniform(streams_of[6], (NVIRT,), jnp.float32, 0.1, 3.0), 0.1, 3.0),
        "frequency": jnp.clip(jnp.exp(jax.random.uniform(streams_of[7], (1,), jnp.float32, math.log(0.2), math.log(2.0))), 0.2, 2.0),
    }


def reference(ri_blocks, blk_occ, blk_virt, live_count, aux_mask, occ_energy, virt_energy, frequency):
    virt_table = virt_energy.reshape(NVB, VBLK)
    energy_gap = virt_table[blk_virt] - occ_energy[blk_occ][:, None]
    is_live = lax.broadcasted_iota(jnp.int32, energy_gap.shape, 1) < live_count[:, None]
    weights = jnp.where(is_live, 2.0 * energy_gap / (energy_gap * energy_gap + frequency[0] * frequency[0]), jnp.zeros_like(energy_gap))
    shaped = ri_blocks.reshape(NBLK, VBLK, NAB, AB)
    kept_blocks = jnp.where(aux_mask[:, None, :, None] == 1, shaped, jnp.zeros_like(shaped)).reshape(NBLK * VBLK, NAUX)
    scaled = (weights.reshape(NBLK * VBLK)[:, None] * kept_blocks).astype(jnp.bfloat16)
    full_matrix = jnp.dot(kept_blocks.T, scaled, preferred_element_type=jnp.float32)
    return full_matrix.reshape(N_AUX, N_OCC, PIECE, NAUX).transpose(1, 0, 2, 3).reshape(NAUX, NAUX)
```

```python
import functools

import jax
import jax.numpy as jnp
from jax import lax
from jax.experimental import pallas as pl
from jax.experimental.pallas import tpu as pltpu
from jax.sharding import PartitionSpec as P

MESH = pl.DeviceIdType.MESH
F32 = jnp.float32
BF16 = jnp.bfloat16


def offset_of(slot):
    return (1 - 2 * (slot % 2)) * ((slot + 1) // 2)


def kernel(
    n, ny, aux_block,
    occ_ids, virt_ids, counts, mask, occ_energy, frequency, virt_ref, x_ref,
    out_ref,
    ga, gb, scaled, rows, wide, virt_rows, meta_shift, meta_count, meta_occ, weight_t,
    recv_a, recv_b, send_sem, y_recv, y_send, p_recv, p_send,
):
    _, depth, cols = x_ref.shape
    half = cols // 2
    run = rows.shape[2]
    far = n // 2
    bundle = n * depth
    o = lax.axis_index("occ")
    a = lax.axis_index("aux")
    z, x = o // n, o % n
    y, core = a // 2, a % 2
    late = z // far

    xp, xm = z * n + (x + 1) % n, z * n + (x + n - 1) % n
    zp, zm = ((z + 1) % n) * n + x, ((z + n - 1) % n) * n + x
    partner = y * 2 + (1 - core)

    barrier = pltpu.get_barrier_semaphore()
    for dest in (xp, xm, zp, zm):
        pl.semaphore_signal(barrier, inc=1, device_id=(dest, a), device_id_type=MESH)
    for d in range(1, ny):
        pl.semaphore_signal(
            barrier, inc=1, device_id=(o, ((y + d) % ny) * 2 + core), device_id_type=MESH
        )
    pl.semaphore_signal(barrier, inc=1, device_id=(o, partner), device_id_type=MESH)

    per_half = half // aux_block
    for k in range(2 * per_half):
        live = mask[o, a * 2 * per_half + k] == 1
        part = x_ref[0, :, k * aux_block:(k + 1) * aux_block]
        part = jnp.where(live, part, jnp.zeros_like(part))
        target, at = (ga, k) if k < per_half else (gb, k - per_half)
        target[0, 0, :, at * aux_block:(at + 1) * aux_block] = part

    pl.semaphore_wait(barrier, 4 + ny - 1 + 1)

    def left(d):
        return 2 * d - 1

    def right(d):
        return 2 * d if d < far else n - 1

    def hop(buf, recv, kind, src, dst, dest):
        pltpu.make_async_remote_copy(
            src_ref=buf.at[src],
            dst_ref=buf.at[dst],
            send_sem=send_sem.at[kind],
            recv_sem=recv.at[dst],
            device_id=(dest, a),
            device_id_type=MESH,
        ).start()

    def arrived(buf, recv, slot):
        pltpu.make_async_copy(buf.at[slot], buf.at[slot], recv.at[slot]).wait()

    plans = (
        (ga, recv_a, 0, zp, zm, far, far - 1, xp, xm),
        (gb, recv_b, 4, xp, xm, far - 1, far, zp, zm),
    )

    def spread(plan, i):
        buf, recv, kind, _, _, _, _, onward, backward = plan
        hop(buf, recv, kind + 2, (0, i), (left(1), i), onward)
        hop(buf, recv, kind + 3, (0, i), (right(1), i), backward)

    for plan in plans:
        buf, recv, kind, up, down = plan[:5]
        hop(buf, recv, kind, (0, 0), (0, left(1)), up)
        hop(buf, recv, kind + 1, (0, 0), (0, right(1)), down)
    for plan in plans:
        spread(plan, 0)

    def fetch(p, carry):
        oj, oi = offset_of(p // n), offset_of(p % n)
        bz = (z + oi + late * (oj - oi) + n) % n
        bx = (x + oj + late * (oi - oj) + n) % n
        b = bz * n + bx
        first = virt_ids[b] * depth
        line = first // 128
        virt_rows[0, pl.ds(p, 1), :] = virt_ref[pl.ds(line, 1), :]
        virt_rows[1, pl.ds(p, 1), :] = virt_ref[
            pl.ds(jnp.minimum(line + 1, virt_ref.shape[0] - 1), 1), :
        ]
        meta_shift[pl.ds(p, 1), :] = jnp.full((1, 128), first - line * 128, jnp.int32)
        meta_count[pl.ds(p, 1), :] = jnp.full((1, 128), counts[b], jnp.int32)
        meta_occ[pl.ds(p, 1), :] = jnp.full((1, 128), occ_energy[occ_ids[b]], F32)
        return carry

    lax.fori_loop(0, n * n, fetch, 0)
    shift = meta_shift[...]
    energy = jnp.zeros(shift.shape, F32)
    pairs = jnp.concatenate([virt_rows[0], virt_rows[1]], axis=1)
    for k in range(8):
        energy = jnp.where(shift == 16 * k, pairs[:, 16 * k:16 * k + 128], energy)
    gap = energy - meta_occ[...]
    freq = frequency[0]
    lane = lax.broadcasted_iota(jnp.int32, shift.shape, 1)
    weight = jnp.where(
        lane < meta_count[...], 2.0 * gap / (gap * gap + freq * freq), jnp.zeros_like(gap)
    )
    weight = jnp.concatenate([weight, jnp.zeros((128 - n * n, 128), F32)], axis=0)
    weight_t[...] = weight.T
    for p in range(n * n):
        wide[p * depth:(p + 1) * depth, :] = jnp.broadcast_to(
            weight_t[0:depth, p:p + 1], (depth, 128)
        )

    for d in range(1, far + 1):
        for plan in plans:
            buf, recv, kind, up, down, up_limit, down_limit = plan[:7]
            if d <= up_limit:
                arrived(buf, recv, (0, left(d)))
                if d < up_limit:
                    hop(buf, recv, kind, (0, left(d)), (0, left(d + 1)), up)
                spread(plan, left(d))
            if d <= down_limit:
                arrived(buf, recv, (0, right(d)))
                if d < down_limit:
                    hop(buf, recv, kind + 1, (0, right(d)), (0, right(d + 1)), down)
                spread(plan, right(d))

    def scale(which, j, i):
        buf = (ga, gb)[which]
        in_order = j * n + i
        swapped = i * n + j
        swap = late if which == 0 else 1 - late
        row = pl.multiple_of((in_order + swap * (swapped - in_order)) * depth, 16)
        w = wide[pl.ds(row, depth), :]
        for t in range(half // 128):
            piece = buf[j, i, :, t * 128:(t + 1) * 128].astype(F32)
            start = which * half + t * 128
            scaled[pl.ds(row, depth), start:start + 128] = (w * piece).astype(BF16)

    tile = pl.multiple_of((o % (n * n // 2)) * run // 128 * 128, 128)
    pick = (
        lax.broadcasted_iota(jnp.int32, (run, 128), 1)
        == lax.broadcasted_iota(jnp.int32, (run, 128), 0) + (o * run) % 128
    ).astype(BF16)

    def slots_of(s):
        return (0, 1) if s == 0 else ((2 * s - 1, 2 * s + 1) if s < far else (n - 1, n))

    def lanes_of(s):
        first, last = slots_of(s)
        return slice(first * bundle, last * bundle)

    def cut(s):
        first, last = slots_of(s)
        for j in range(first, last):
            from_a = ga[j, :, :, pl.ds(tile, 128)].reshape(bundle, 128)
            from_b = gb[j, :, :, pl.ds(tile, 128)].reshape(bundle, 128)
            block = jnp.where(late == 1, from_b, from_a)
            slab = lax.dot_general(
                pick, block, (((1,), (1,)), ((), ())), preferred_element_type=F32
            )
            rows[y, core, :, j * bundle:(j + 1) * bundle] = slab.astype(BF16)
        mine = rows.at[y, core, :, lanes_of(s)]
        for d in range(1, ny):
            pltpu.make_async_remote_copy(
                src_ref=mine,
                dst_ref=mine,
                send_sem=y_send.at[s],
                recv_sem=y_recv.at[s],
                device_id=(o, ((y + d) % ny) * 2 + core),
                device_id_type=MESH,
            ).start()

    def others(s):
        return rows.at[0:ny - 1, 0, :, lanes_of(s)]

    def pass_on(s):
        pltpu.make_async_copy(others(s), others(s), y_recv.at[s]).wait()
        ours = rows.at[:, core, :, lanes_of(s)]
        pltpu.make_async_remote_copy(
            src_ref=ours,
            dst_ref=ours,
            send_sem=p_send.at[s],
            recv_sem=p_recv.at[s],
            device_id=(o, partner),
            device_id_type=MESH,
        ).start()

    def rows_here(s):
        theirs = rows.at[:, 1 - core, :, lanes_of(s)]
        pltpu.make_async_copy(theirs, theirs, p_recv.at[s]).wait()

    n_rows = out_ref.shape[0]
    tile_n = min(256, half)

    def multiply(which, s, fresh):
        k = lanes_of(s)

        def body(t, carry):
            at = pl.ds(pl.multiple_of(which * half + t * tile_n, 128), tile_n)
            part = jnp.dot(
                rows[:, :, :, k].reshape(n_rows, k.stop - k.start),
                scaled[k, at],
                preferred_element_type=F32,
            )
            if fresh:
                out_ref[:, at] = part
            else:
                out_ref[:, at] += part
            return carry

        lax.fori_loop(0, half // tile_n, body, 0)

    def own_units(i, carry):
        scale(0, 0, i)
        scale(1, 0, i)
        return carry

    lax.fori_loop(0, n, own_units, 0)
    cut(0)
    for s in range(1, far + 1):
        def pair(i2, carry):
            for parity in range(2):
                i = 2 * i2 + parity
                for which, plan in enumerate(plans):
                    buf, recv, kind = plan[:3]
                    onward, backward = plan[7:]
                    up_limit, down_limit = far - parity, far - 1 + parity
                    if s <= up_limit:
                        arrived(buf, recv, (left(s), i))
                        if s < up_limit:
                            hop(buf, recv, kind + 2, (left(s), i), (left(s + 1), i), onward)
                    if s <= down_limit:
                        arrived(buf, recv, (right(s), i))
                        if s < down_limit:
                            hop(buf, recv, kind + 3, (right(s), i), (right(s + 1), i), backward)
                for which in range(2):
                    if s <= up_limit:
                        scale(which, left(s), i)
                    if s <= down_limit:
                        scale(which, right(s), i)
            return carry

        lax.fori_loop(0, n // 2, pair, 0)
        cut(s)
        pass_on(s - 1)
        if s >= 2:
            rows_here(s - 2)
            multiply(late, s - 2, s == 2)
    rows_here(far - 1)
    multiply(late, far - 1, False)
    for s in range(far):
        multiply(1 - late, s, s == 0)
    pass_on(far)
    rows_here(far)
    multiply(late, far, False)
    multiply(1 - late, far, False)

    for plan in plans:
        buf, _, kind, _, _, up_limit, down_limit, _, _ = plan
        flat = ((kind, up_limit), (kind + 1, down_limit))
        for sem, count in flat:
            sent = buf.at[0, 0:count]
            pltpu.make_async_copy(sent, sent, send_sem.at[sem]).wait()
        for sem in (kind + 2, kind + 3):
            sent = buf.at[0:n - 1, 0:n // 2]
            pltpu.make_async_copy(sent, sent, send_sem.at[sem]).wait()
    for s in range(far + 1):
        pltpu.make_async_copy(others(s), others(s), y_send.at[s]).wait()
        ours = rows.at[:, core, :, lanes_of(s)]
        pltpu.make_async_copy(ours, ours, p_send.at[s]).wait()


def solution(mesh):
    n = 1
    while n * n < mesh.shape["occ"]:
        n += 1
    ny = mesh.shape["aux"] // 2
    far = n // 2

    def per_device(ri, occ_ids, virt_ids, counts, mask, occ_energy, virt_energy, frequency):
        _, depth, cols = ri.shape
        run = cols // (n * n)
        n_rows = 2 * ny * run
        total = n * n * depth
        aux_block = cols * 2 * ny // mask.shape[1]
        smem = pl.BlockSpec(memory_space=pltpu.SMEM)
        vmem = pl.BlockSpec(memory_space=pltpu.VMEM)
        return pl.pallas_call(
            functools.partial(kernel, n, ny, aux_block),
            out_shape=jax.ShapeDtypeStruct((n_rows, cols), F32),
            in_specs=[smem] * 6 + [vmem] * 2,
            out_specs=vmem,
            scratch_shapes=[
                pltpu.VMEM((n, n, depth, cols // 2), BF16),
                pltpu.VMEM((n, n, depth, cols // 2), BF16),
                pltpu.VMEM((total, cols), BF16),
                pltpu.VMEM((ny, 2, run, total), BF16),
                pltpu.VMEM((total, 128), F32),
                pltpu.VMEM((2, n * n, 128), F32),
                pltpu.VMEM((n * n, 128), jnp.int32),
                pltpu.VMEM((n * n, 128), jnp.int32),
                pltpu.VMEM((n * n, 128), F32),
                pltpu.VMEM((128, 128), F32),
                pltpu.SemaphoreType.DMA((n, n)),
                pltpu.SemaphoreType.DMA((n, n)),
                pltpu.SemaphoreType.DMA((8,)),
                pltpu.SemaphoreType.DMA((far + 1,)),
                pltpu.SemaphoreType.DMA((far + 1,)),
                pltpu.SemaphoreType.DMA((far + 1,)),
                pltpu.SemaphoreType.DMA((far + 1,)),
            ],
            compiler_params=pltpu.CompilerParams(
                collective_id=0, has_side_effects=True, vmem_limit_bytes=48 * 1024 * 1024
            ),
            name="response",
        )(
            occ_ids, virt_ids, counts, mask, occ_energy, frequency,
            virt_energy.reshape(-1, 128), ri,
        )

    placed = (P("occ", None, "aux"), P(), P(), P(), P(), P(), P(), P())
    return jax.shard_map(
        per_device, mesh=mesh, in_specs=placed, out_specs=P("occ", "aux"), check_vma=False
    )
```

```python
import functools

import jax
import jax.numpy as jnp
from jax import lax
from jax.experimental import pallas as pl
from jax.experimental.pallas import tpu as pltpu
from jax.sharding import PartitionSpec as P

MESH = pl.DeviceIdType.MESH
F32 = jnp.float32
BF16 = jnp.bfloat16
POINTS = (0, 6, 10)
MOST = 13


def offset_of(slot):
    return (1 - 2 * (slot % 2)) * ((slot + 1) // 2)


def kernel(
    n, ny, aux_block,
    occ_ids_in, virt_ids_in, counts_in, mask_in, occ_energy_in, frequency_in, virt_in, x_in,
    out_ref,
    ga, gb, scaled, last, rows, tail, mine, tiles, runs, wide,
    occ_ids, virt_ids, counts, occ_energy, frequency, mask, virt,
    virt_rows, meta_shift, meta_count, meta_occ, weight_t,
    recv_a, recv_b, send_sem, load_sem, t_recv, t_send, r_recv, r_send,
    y_recv, y_send, p_recv, p_send,
):
    depth, half = ga.shape[2:]
    run = rows.shape[3]
    far = n // 2
    bundle = n * depth
    o = lax.axis_index("occ")
    a = lax.axis_index("aux")
    z, x = o // n, o % n
    y, core = a // 2, a % 2

    def at_x(d):
        return z * n + (x + d + n) % n

    def at_z(d):
        return ((z + d + n) % n) * n + x

    def at_y(d):
        return (y + d + ny) % ny

    xp, xm, zp, zm = at_x(1), at_x(-1), at_z(1), at_z(-1)
    partner = y * 2 + (1 - core)
    near = sorted({d % ny for d in (1, -1, 2, -2)} - {0})

    loads = [
        pltpu.make_async_copy(src, dst, load_sem.at[k])
        for k, (src, dst) in enumerate((
            (mask_in, mask),
            (x_in.at[0, :, 0:half], ga.at[0, 0]),
            (x_in.at[0, :, half:2 * half], gb.at[0, 0]),
            (occ_ids_in, occ_ids),
            (virt_ids_in, virt_ids),
            (counts_in, counts),
            (occ_energy_in, occ_energy),
            (frequency_in, frequency),
            (virt_in, virt),
        ))
    ]
    for load in loads:
        load.start()

    barrier = pltpu.get_barrier_semaphore()
    for d in range(1, n):
        for dest in (at_x(d), at_z(d)):
            pl.semaphore_signal(barrier, inc=1, device_id=(dest, a), device_id_type=MESH)
    for d in near:
        pl.semaphore_signal(
            barrier, inc=1, device_id=(o, at_y(d) * 2 + core), device_id_type=MESH
        )
    pl.semaphore_signal(barrier, inc=1, device_id=(o, partner), device_id_type=MESH)

    for load in loads[:3]:
        load.wait()
    mask_row = mask[pl.ds(o, 1), :]
    mask_lane = lax.broadcasted_iota(jnp.int32, mask_row.shape, 1)
    per_half = half // aux_block
    for k in range(2 * per_half):
        live = jnp.sum(
            jnp.where(mask_lane == a * 2 * per_half + k, mask_row, 0), axis=1, keepdims=True
        )
        target, at = (ga, k) if k < per_half else (gb, k - per_half)
        place = slice(at * aux_block, (at + 1) * aux_block)
        part = target[0, 0, :, place]
        keep = jnp.broadcast_to(live, part.shape) == 1
        part = jnp.where(keep, part, jnp.zeros_like(part))
        target[0, 0, :, place] = part
        for t in range(max(1, aux_block // 128)):
            if aux_block >= 128:
                mine[k * aux_block // 128 + t] = part[:, t * 128:(t + 1) * 128]
            else:
                low = k * aux_block % 128
                mine[k * aux_block // 128, :, low:low + aux_block] = part

    pl.semaphore_wait(barrier, 2 * (n - 1) + len(near) + 1)

    def left(d):
        return 2 * d - 1

    def right(d):
        return 2 * d if d < far else n - 1

    def remote(src, dst, send, recv, dest):
        pltpu.make_async_remote_copy(
            src_ref=src, dst_ref=dst, send_sem=send, recv_sem=recv,
            device_id=dest, device_id_type=MESH,
        ).start()

    def settle(ref, sem):
        pltpu.make_async_copy(ref, ref, sem).wait()

    def hop(buf, recv, kind, src, dst, dest):
        remote(buf.at[src], buf.at[dst], send_sem.at[kind], recv.at[dst], (dest, a))

    def arrived(buf, recv, slot):
        settle(buf.at[slot], recv.at[slot])

    plans = (
        (ga, recv_a, 0, zp, zm, far, far - 1, xp, xm),
        (gb, recv_b, 4, xp, xm, far - 1, far, zp, zm),
    )

    def spread(plan, i):
        buf, recv, kind, _, _, _, _, onward, backward = plan
        hop(buf, recv, kind + 2, (0, i), (left(1), i), onward)
        hop(buf, recv, kind + 3, (0, i), (right(1), i), backward)

    for plan in plans:
        buf, recv, kind, up, down = plan[:5]
        hop(buf, recv, kind, (0, 0), (0, left(1)), up)
        hop(buf, recv, kind + 1, (0, 0), (0, right(1)), down)
    own_tile = z * n * run // 128
    for j in range(1, n):
        k = (z - offset_of(j) + n) % n
        remote(mine.at[k * n * run // 128], tiles.at[j], t_send, t_recv, (k * n + x, a))
    tiles[0] = mine[own_tile]
    for plan in plans:
        spread(plan, 0)

    def fetch(p, carry):
        oj, oi = offset_of(p // n), offset_of(p % n)
        b = ((z + oi + n) % n) * n + (x + oj + n) % n
        first = virt_ids[b] * depth
        line = first // 128
        virt_rows[0, pl.ds(p, 1), :] = virt[pl.ds(line, 1), :]
        virt_rows[1, pl.ds(p, 1), :] = virt[pl.ds(jnp.minimum(line + 1, virt.shape[0] - 1), 1), :]
        meta_shift[pl.ds(p, 1), :] = jnp.full((1, 128), first - line * 128, jnp.int32)
        meta_count[pl.ds(p, 1), :] = jnp.full((1, 128), counts[b], jnp.int32)
        meta_occ[pl.ds(p, 1), :] = jnp.full((1, 128), occ_energy[occ_ids[b]], F32)
        return carry

    def cut():
        settle(tiles.at[1:n], t_recv)
        lane = lax.broadcasted_iota(jnp.int32, (128, 128), 1)
        line = lax.broadcasted_iota(jnp.int32, (128, 128), 0)
        pick = (lane == line + z * n * run % 128).astype(BF16)
        block = tiles[...].reshape(bundle, 128)
        turned = lax.dot_general(
            pick, block, (((1,), (1,)), ((), ())), preferred_element_type=F32
        ).astype(BF16)
        runs[...] = turned[0:n * run].reshape(runs.shape)
        for j in range(1, n):
            k = (x - offset_of(j) + n) % n
            remote(runs.at[k], rows.at[y, core, j], r_send, r_recv, (z * n + k, a))
        rows[y, core, 0] = runs[x]

    for load in loads[3:]:
        load.wait()
    for d in range(1, far + 1):
        landed = []
        for plan in plans:
            buf, recv, kind, up, down, up_limit, down_limit = plan[:7]
            if d <= up_limit:
                arrived(buf, recv, (0, left(d)))
                if d < up_limit:
                    hop(buf, recv, kind, (0, left(d)), (0, left(d + 1)), up)
                landed.append((plan, left(d)))
            if d <= down_limit:
                arrived(buf, recv, (0, right(d)))
                if d < down_limit:
                    hop(buf, recv, kind + 1, (0, right(d)), (0, right(d + 1)), down)
                landed.append((plan, right(d)))
        for plan, i in landed:
            spread(plan, i)
        if d == 1:
            cut()
        if d < far:
            share = -(-n * n // (far - 1))
            lax.fori_loop(share * (d - 1), min(share * d, n * n), fetch, 0)

    shift = meta_shift[...]
    energy = jnp.zeros(shift.shape, F32)
    both = jnp.concatenate([virt_rows[0], virt_rows[1]], axis=1)
    for k in range(8):
        energy = jnp.where(shift == 16 * k, both[:, 16 * k:16 * k + 128], energy)
    gap = energy - meta_occ[...]
    freq = frequency[0]
    weight = jnp.where(
        lax.broadcasted_iota(jnp.int32, shift.shape, 1) < meta_count[...],
        2.0 * gap / (gap * gap + freq * freq),
        jnp.zeros_like(gap),
    )
    weight = jnp.concatenate([weight, jnp.zeros((128 - n * n, 128), F32)], axis=0)
    weight_t[...] = weight.T
    for p in range(n * n):
        wide[p * depth:(p + 1) * depth, :] = jnp.broadcast_to(
            weight_t[0:depth, p:p + 1], (depth, 128)
        )

    def order(which, j, i):
        return j * n + i if which == 0 else i * n + j

    def scale(which, j, i, apart=False):
        buf = (ga, gb)[which]
        row = pl.multiple_of(order(which, j, i) * depth, 16)
        w = wide[pl.ds(row, depth), :]
        for t in range(half // 128):
            place = slice(t * 128, (t + 1) * 128)
            piece = (w * buf[j, i, :, place].astype(F32)).astype(BF16)
            if apart:
                last[which, pl.ds(pl.multiple_of(i * depth, 16), depth), place] = piece
            else:
                scaled[which, pl.ds(row, depth), place] = piece

    def own_slab(d):
        return rows.at[at_y(d), core]

    def pass_slab(d, by):
        remote(
            own_slab(d), own_slab(d), y_send, y_recv.at[(d - by) % ny],
            (o, at_y(by) * 2 + core),
        )

    def to_partner(d):
        remote(own_slab(d), own_slab(d), p_send, p_recv, (o, partner))

    relay = ((-1, 2), (1, -2), (-2, 2)) if ny > 5 else ()

    def ring_point(stage):
        if stage == 0:
            settle(rows.at[0, 0, 0:n - 1], r_recv)
            for d in near:
                pass_slab(0, d)
            to_partner(0)
        elif stage == 1:
            for d in near:
                settle(own_slab(d), y_recv.at[d])
            for d, by in relay:
                pass_slab(d, by)
            for d in near:
                to_partner(d)
        else:
            for d, by in relay:
                settle(own_slab(d - by), y_recv.at[(d - by) % ny])
                to_partner(d - by)

    n_rows = out_ref.shape[0]
    tile_n = min(256, half)

    def each_tile(body):
        lax.fori_loop(0, half // tile_n, lambda t, c: (body(t), c)[1], 0)

    def multiply_most(which):
        def body(t):
            part = pl.ds(pl.multiple_of(t * tile_n, 128), tile_n)

            to = pl.ds(pl.multiple_of(which * half + t * tile_n, 128), tile_n)
            for j in range(0, n, 2):
                pair_of = [rows[:, :, j + k].reshape(n_rows, bundle) for k in range(2)]
                part_sum = jnp.dot(
                    jnp.concatenate(pair_of, axis=1),
                    scaled[which, j * bundle:(j + 2) * bundle, part],
                    preferred_element_type=F32,
                )
                if j == 0:
                    out_ref[:, to] = part_sum
                else:
                    out_ref[:, to] += part_sum

        each_tile(body)

    def multiply_last(which):
        def body(t):
            part = pl.ds(pl.multiple_of(t * tile_n, 128), tile_n)
            to = pl.ds(pl.multiple_of(which * half + t * tile_n, 128), tile_n)
            out_ref[:, to] += jnp.dot(
                tail[which], last[which, :, part], preferred_element_type=F32
            )

        each_tile(body)

    def own_units(i, carry):
        scale(0, 0, i)
        scale(1, 0, i)
        return carry

    lax.fori_loop(0, n, own_units, 0)
    for which in range(2):
        for i in range(n):
            row = pl.multiple_of(order(which, n - 1, i) * depth, 16)
            scaled[which, pl.ds(row, depth), :] = jnp.zeros((depth, half), BF16)

    def second(s, first, stop):
        def pair(i2, carry):
            for parity in range(2):
                i = 2 * i2 + parity
                up_limit, down_limit = far - parity, far - 1 + parity
                for plan in plans:
                    buf, recv, kind = plan[:3]
                    onward, backward = plan[7:]
                    if s <= up_limit:
                        arrived(buf, recv, (left(s), i))
                        if s < up_limit:
                            hop(buf, recv, kind + 2, (left(s), i), (left(s + 1), i), onward)
                    if s <= down_limit:
                        arrived(buf, recv, (right(s), i))
                        if s < down_limit:
                            hop(buf, recv, kind + 3, (right(s), i), (right(s + 1), i), backward)
            for parity in range(2):
                i = 2 * i2 + parity
                up_limit, down_limit = far - parity, far - 1 + parity
                for which in range(2):
                    if s <= up_limit:
                        scale(which, left(s), i, s == far)
                    if s <= down_limit:
                        scale(which, right(s), i, s == far)
            return carry

        lax.fori_loop(first, stop, pair, 0)

    pairs_of = n // 2
    points, most = (POINTS, MOST) if n == 8 else ((0, 1, 2), 3)
    stops = {points[1]: 1, points[2]: 2}
    ring_point(0)
    for s in range(1, far + 1):
        first = 0
        for stop in range(1, pairs_of + 1):
            count = (s - 1) * pairs_of + stop
            if stop == pairs_of or count in stops or count == most:
                second(s, first, stop)
                first = stop
            if count in stops:
                ring_point(stops[count])
            if count == most:
                settle(rows.at[:, 1 - core], p_recv)
                tail[0] = rows[:, :, n - 1].reshape(n_rows, bundle)
                tail[1] = jnp.concatenate(
                    [
                        rows[:, :, i].reshape(n_rows, bundle)[:, (n - 1) * depth:]
                        for i in range(n)
                    ],
                    axis=1,
                )
                multiply_most(0)
                multiply_most(1)
    multiply_last(0)
    multiply_last(1)

    for plan in plans:
        buf, _, kind, _, _, up_limit, down_limit, _, _ = plan
        settle(buf.at[0, 0:up_limit], send_sem.at[kind])
        settle(buf.at[0, 0:down_limit], send_sem.at[kind + 1])
        for sem in (kind + 2, kind + 3):
            settle(buf.at[0:n - 1, 0:n // 2], send_sem.at[sem])

    settle(tiles.at[1:n], t_send)
    settle(runs.at[1:n], r_send)
    settle(rows.at[0:ny - 1, 0], y_send)
    settle(rows.at[:, core], p_send)


def solution(mesh):
    n = 1
    while n * n < mesh.shape["occ"]:
        n += 1
    ny = mesh.shape["aux"] // 2

    def per_device(ri, occ_ids, virt_ids, counts, mask, occ_energy, virt_energy, frequency):
        _, depth, cols = ri.shape
        run = cols // (n * n)
        n_rows = 2 * ny * run
        total = n * n * depth
        half = cols // 2
        aux_block = cols * 2 * ny // mask.shape[1]
        virt = virt_energy.reshape(-1, 128)
        dma = pltpu.SemaphoreType.DMA
        return pl.pallas_call(
            functools.partial(kernel, n, ny, aux_block),
            out_shape=jax.ShapeDtypeStruct((n_rows, cols), F32),
            in_specs=[pl.BlockSpec(memory_space=pltpu.HBM)] * 8,
            out_specs=pl.BlockSpec(memory_space=pltpu.VMEM),
            scratch_shapes=[
                pltpu.VMEM((n, n, depth, half), BF16),
                pltpu.VMEM((n, n, depth, half), BF16),
                pltpu.VMEM((2, total, half), BF16),
                pltpu.VMEM((2, n * depth, half), BF16),
                pltpu.VMEM((ny, 2, n, run, n * depth), BF16),
                pltpu.VMEM((2, n_rows, n * depth), BF16),
                pltpu.VMEM((cols // 128, depth, 128), BF16),
                pltpu.VMEM((n, depth, 128), BF16),
                pltpu.VMEM((n, run, n * depth), BF16),
                pltpu.VMEM((total, 128), F32),
                pltpu.SMEM(occ_ids.shape, jnp.int32),
                pltpu.SMEM(virt_ids.shape, jnp.int32),
                pltpu.SMEM(counts.shape, jnp.int32),
                pltpu.SMEM(occ_energy.shape, F32),
                pltpu.SMEM(frequency.shape, F32),
                pltpu.VMEM(mask.shape, jnp.int32),
                pltpu.VMEM(virt.shape, F32),
                pltpu.VMEM((2, n * n, 128), F32),
                pltpu.VMEM((n * n, 128), jnp.int32),
                pltpu.VMEM((n * n, 128), jnp.int32),
                pltpu.VMEM((n * n, 128), F32),
                pltpu.VMEM((128, 128), F32),
                dma((n, n)), dma((n, n)), dma((8,)), dma((9,)),
                dma, dma, dma, dma, dma((ny,)), dma, dma, dma,
            ],
            compiler_params=pltpu.CompilerParams(
                collective_id=0, has_side_effects=True, vmem_limit_bytes=60 * 1024 * 1024
            ),
            name="response",
        )(occ_ids, virt_ids, counts, mask, occ_energy, frequency, virt, ri)

    placed = (P("occ", None, "aux"), P(), P(), P(), P(), P(), P(), P())
    return jax.shard_map(
        per_device, mesh=mesh, in_specs=placed, out_specs=P("occ", "aux"), check_vma=False
    )
```

```python
import functools

import jax
import jax.numpy as jnp
from jax import lax
from jax.experimental import pallas as pl
from jax.experimental.pallas import tpu as pltpu
from jax.sharding import PartitionSpec as P

MESH = pl.DeviceIdType.MESH
F32 = jnp.float32
BF16 = jnp.bfloat16
POINTS = (0, 6, 10)
MOST = 13


def offset_of(slot):
    return (1 - 2 * (slot % 2)) * ((slot + 1) // 2)


def kernel(
    n, ny, aux_block,
    occ_ids_in, virt_ids_in, counts_in, mask_in, occ_energy_in, frequency_in, virt_in, x_in,
    out_ref,
    ga, gb, scaled, last, rows, tail, mine, tiles, runs, wide,
    occ_ids, virt_ids, counts, occ_energy, frequency, mask, virt,
    virt_rows, meta_shift, meta_count, meta_occ, weight_t,
    recv_a, recv_b, send_sem, load_sem, t_recv, t_send, r_recv, r_send,
    y_recv, y_send, p_recv, p_send,
):
    depth, half = ga.shape[2:]
    run = rows.shape[3]
    far = n // 2
    bundle = n * depth
    o = lax.axis_index("occ")
    a = lax.axis_index("aux")
    z, x = o // n, o % n
    y, core = a // 2, a % 2

    def at_x(d):
        return z * n + (x + d + n) % n

    def at_z(d):
        return ((z + d + n) % n) * n + x

    def at_y(d):
        return (y + d + ny) % ny

    xp, xm, zp, zm = at_x(1), at_x(-1), at_z(1), at_z(-1)
    partner = y * 2 + (1 - core)
    near = sorted({d % ny for d in (1, -1, 2, -2)} - {0})

    loads = [
        pltpu.make_async_copy(src, dst, load_sem.at[k])
        for k, (src, dst) in enumerate((
            (mask_in, mask),
            (x_in.at[0, :, 0:half], ga.at[0, 0]),
            (x_in.at[0, :, half:2 * half], gb.at[0, 0]),
            (occ_ids_in, occ_ids),
            (virt_ids_in, virt_ids),
            (counts_in, counts),
            (occ_energy_in, occ_energy),
            (frequency_in, frequency),
            (virt_in, virt),
        ))
    ]
    for load in loads:
        load.start()

    barrier = pltpu.get_barrier_semaphore()
    for d in range(1, n):
        for dest in (at_x(d), at_z(d)):
            pl.semaphore_signal(barrier, inc=1, device_id=(dest, a), device_id_type=MESH)
    for d in near:
        pl.semaphore_signal(
            barrier, inc=1, device_id=(o, at_y(d) * 2 + core), device_id_type=MESH
        )
    pl.semaphore_signal(barrier, inc=1, device_id=(o, partner), device_id_type=MESH)

    for load in loads[:3]:
        load.wait()
    mask_row = mask[pl.ds(o, 1), :]
    mask_lane = lax.broadcasted_iota(jnp.int32, mask_row.shape, 1)
    per_half = half // aux_block
    for k in range(2 * per_half):
        live = jnp.sum(
            jnp.where(mask_lane == a * 2 * per_half + k, mask_row, 0), axis=1, keepdims=True
        )
        target, at = (ga, k) if k < per_half else (gb, k - per_half)
        place = slice(at * aux_block, (at + 1) * aux_block)
        part = target[0, 0, :, place]
        keep = jnp.broadcast_to(live, part.shape) == 1
        part = jnp.where(keep, part, jnp.zeros_like(part))
        target[0, 0, :, place] = part
        for t in range(max(1, aux_block // 128)):
            if aux_block >= 128:
                mine[k * aux_block // 128 + t] = part[:, t * 128:(t + 1) * 128]
            else:
                low = k * aux_block % 128
                mine[k * aux_block // 128, :, low:low + aux_block] = part

    pl.semaphore_wait(barrier, 2 * (n - 1) + len(near) + 1)

    def left(d):
        return 2 * d - 1

    def right(d):
        return 2 * d if d < far else n - 1

    def remote(src, dst, send, recv, dest):
        pltpu.make_async_remote_copy(
            src_ref=src, dst_ref=dst, send_sem=send, recv_sem=recv,
            device_id=dest, device_id_type=MESH,
        ).start()

    def settle(ref, sem):
        pltpu.make_async_copy(ref, ref, sem).wait()

    def hop(buf, recv, kind, src, dst, dest):
        remote(buf.at[src], buf.at[dst], send_sem.at[kind], recv.at[dst], (dest, a))

    def arrived(buf, recv, slot):
        settle(buf.at[slot], recv.at[slot])

    plans = (
        (ga, recv_a, 0, zp, zm, far, far - 1, xp, xm),
        (gb, recv_b, 4, xp, xm, far, far - 1, zp, zm),
    )

    def spread(plan, i):
        buf, recv, kind, _, _, _, _, onward, backward = plan
        hop(buf, recv, kind + 2, (0, i), (left(1), i), onward)
        hop(buf, recv, kind + 3, (0, i), (right(1), i), backward)

    for plan in plans:
        buf, recv, kind, up, down = plan[:5]
        hop(buf, recv, kind, (0, 0), (0, left(1)), up)
        hop(buf, recv, kind + 1, (0, 0), (0, right(1)), down)
    own_tile = z * n * run // 128
    for j in range(1, n):
        k = (z - offset_of(j) + n) % n
        remote(mine.at[k * n * run // 128], tiles.at[j], t_send, t_recv, (k * n + x, a))
    tiles[0] = mine[own_tile]
    for plan in plans:
        spread(plan, 0)

    def fetch(p, carry):
        oj, oi = offset_of(p // n), offset_of(p % n)
        b = ((z + oi + n) % n) * n + (x + oj + n) % n
        first = virt_ids[b] * depth
        line = first // 128
        virt_rows[0, pl.ds(p, 1), :] = virt[pl.ds(line, 1), :]
        virt_rows[1, pl.ds(p, 1), :] = virt[pl.ds(jnp.minimum(line + 1, virt.shape[0] - 1), 1), :]
        meta_shift[pl.ds(p, 1), :] = jnp.full((1, 128), first - line * 128, jnp.int32)
        meta_count[pl.ds(p, 1), :] = jnp.full((1, 128), counts[b], jnp.int32)
        meta_occ[pl.ds(p, 1), :] = jnp.full((1, 128), occ_energy[occ_ids[b]], F32)
        return carry

    def cut():
        settle(tiles.at[1:n], t_recv)
        lane = lax.broadcasted_iota(jnp.int32, (128, 128), 1)
        line = lax.broadcasted_iota(jnp.int32, (128, 128), 0)
        pick = (lane == line + z * n * run % 128).astype(BF16)
        block = tiles[...].reshape(bundle, 128)
        turned = lax.dot_general(
            pick, block, (((1,), (1,)), ((), ())), preferred_element_type=F32
        ).astype(BF16)
        runs[...] = turned[0:n * run].reshape(runs.shape)
        for j in range(1, n):
            k = (x - offset_of(j) + n) % n
            remote(runs.at[k], rows.at[y, core, j], r_send, r_recv, (z * n + k, a))
        rows[y, core, 0] = runs[x]

    for load in loads[3:]:
        load.wait()
    for d in range(1, far + 1):
        landed = []
        for plan in plans:
            buf, recv, kind, up, down, up_limit, down_limit = plan[:7]
            if d <= up_limit:
                arrived(buf, recv, (0, left(d)))
                if d < up_limit:
                    hop(buf, recv, kind, (0, left(d)), (0, left(d + 1)), up)
                landed.append((plan, left(d)))
            if d <= down_limit:
                arrived(buf, recv, (0, right(d)))
                if d < down_limit:
                    hop(buf, recv, kind + 1, (0, right(d)), (0, right(d + 1)), down)
                landed.append((plan, right(d)))
        for plan, i in landed:
            spread(plan, i)
        if d == 1:
            cut()
        if d < far:
            share = -(-n * n // (far - 1))
            lax.fori_loop(share * (d - 1), min(share * d, n * n), fetch, 0)

    shift = meta_shift[...]
    energy = jnp.zeros(shift.shape, F32)
    both = jnp.concatenate([virt_rows[0], virt_rows[1]], axis=1)
    for k in range(8):
        energy = jnp.where(shift == 16 * k, both[:, 16 * k:16 * k + 128], energy)
    gap = energy - meta_occ[...]
    freq = frequency[0]
    weight = jnp.where(
        lax.broadcasted_iota(jnp.int32, shift.shape, 1) < meta_count[...],
        2.0 * gap / (gap * gap + freq * freq),
        jnp.zeros_like(gap),
    )
    weight = jnp.concatenate([weight, jnp.zeros((128 - n * n, 128), F32)], axis=0)
    weight_t[...] = weight.T
    for p in range(n * n):
        wide[p * depth:(p + 1) * depth, :] = jnp.broadcast_to(
            weight_t[0:depth, p:p + 1], (depth, 128)
        )

    def order(which, j, i):
        return j * n + i if which == 0 else i * n + j

    def scale(which, j, i, apart=False):
        buf = (ga, gb)[which]
        row = pl.multiple_of(order(which, j, i) * depth, 16)
        w = wide[pl.ds(row, depth), :]
        for t in range(half // 128):
            place = slice(t * 128, (t + 1) * 128)
            piece = (w * buf[j, i, :, place].astype(F32)).astype(BF16)
            if apart:
                last[which, pl.ds(pl.multiple_of(i * depth, 16), depth), place] = piece
            else:
                scaled[which, pl.ds(row, depth), place] = piece

    def own_slab(d):
        return rows.at[at_y(d), core]

    def pass_slab(d, by):
        remote(
            own_slab(d), own_slab(d), y_send, y_recv.at[(d - by) % ny],
            (o, at_y(by) * 2 + core),
        )

    def to_partner(d):
        remote(own_slab(d), own_slab(d), p_send, p_recv, (o, partner))

    relay = ((-1, 2), (1, -2), (-2, 2)) if ny > 5 else ()

    def ring_point(stage):
        if stage == 0:
            settle(rows.at[0, 0, 0:n - 1], r_recv)
            for d in near:
                pass_slab(0, d)
            to_partner(0)
        elif stage == 1:
            for d in near:
                settle(own_slab(d), y_recv.at[d])
            for d, by in relay:
                pass_slab(d, by)
            for d in near:
                to_partner(d)
        else:
            for d, by in relay:
                settle(own_slab(d - by), y_recv.at[(d - by) % ny])
                to_partner(d - by)

    n_rows = out_ref.shape[0]
    tile_n = min(256, half)

    def each_tile(body):
        lax.fori_loop(0, half // tile_n, lambda t, c: (body(t), c)[1], 0)

    def multiply_most(which):
        def body(t):
            part = pl.ds(pl.multiple_of(t * tile_n, 128), tile_n)

            to = pl.ds(pl.multiple_of(which * half + t * tile_n, 128), tile_n)
            for j in range(0, n, 2):
                pair_of = [rows[:, :, j + k].reshape(n_rows, bundle) for k in range(2)]
                part_sum = jnp.dot(
                    jnp.concatenate(pair_of, axis=1),
                    scaled[which, j * bundle:(j + 2) * bundle, part],
                    preferred_element_type=F32,
                )
                if j == 0:
                    out_ref[:, to] = part_sum
                else:
                    out_ref[:, to] += part_sum

        each_tile(body)

    def multiply_last(which):
        def body(t):
            part = pl.ds(pl.multiple_of(t * tile_n, 128), tile_n)
            to = pl.ds(pl.multiple_of(which * half + t * tile_n, 128), tile_n)
            out_ref[:, to] += jnp.dot(
                tail[which], last[which, :, part], preferred_element_type=F32
            )

        each_tile(body)

    def own_units(i, carry):
        scale(0, 0, i)
        scale(1, 0, i)
        return carry

    lax.fori_loop(0, n, own_units, 0)
    for which in range(2):
        for i in range(n):
            row = pl.multiple_of(order(which, n - 1, i) * depth, 16)
            scaled[which, pl.ds(row, depth), :] = jnp.zeros((depth, half), BF16)

    def second(s, first, stop):
        def pair(i2, carry):
            for parity in range(2):
                i = 2 * i2 + parity
                up_limit, down_limit = far - parity, far - 1 + parity
                for plan in plans:
                    buf, recv, kind = plan[:3]
                    onward, backward = plan[7:]
                    if s <= up_limit:
                        arrived(buf, recv, (left(s), i))
                        if s < up_limit:
                            hop(buf, recv, kind + 2, (left(s), i), (left(s + 1), i), onward)
                    if s <= down_limit:
                        arrived(buf, recv, (right(s), i))
                        if s < down_limit:
                            hop(buf, recv, kind + 3, (right(s), i), (right(s + 1), i), backward)
            for parity in range(2):
                i = 2 * i2 + parity
                up_limit, down_limit = far - parity, far - 1 + parity
                for which in range(2):
                    if s <= up_limit:
                        scale(which, left(s), i, s == far)
                    if s <= down_limit:
                        scale(which, right(s), i, s == far)
            return carry

        lax.fori_loop(first, stop, pair, 0)

    pairs_of = n // 2
    points, most = (POINTS, MOST) if n == 8 else ((0, 1, 2), 3)
    stops = {points[1]: 1, points[2]: 2}
    ring_point(0)
    for s in range(1, far + 1):
        first = 0
        for stop in range(1, pairs_of + 1):
            count = (s - 1) * pairs_of + stop
            if stop == pairs_of or count in stops or count == most:
                second(s, first, stop)
                first = stop
            if count in stops:
                ring_point(stops[count])
            if count == most:
                settle(rows.at[:, 1 - core], p_recv)
                tail[0] = rows[:, :, n - 1].reshape(n_rows, bundle)
                tail[1] = jnp.concatenate(
                    [
                        rows[:, :, i].reshape(n_rows, bundle)[:, (n - 1) * depth:]
                        for i in range(n)
                    ],
                    axis=1,
                )
                multiply_most(0)
                multiply_most(1)
    multiply_last(0)
    multiply_last(1)

    for plan in plans:
        buf, _, kind, _, _, up_limit, down_limit, _, _ = plan
        settle(buf.at[0, 0:up_limit], send_sem.at[kind])
        settle(buf.at[0, 0:down_limit], send_sem.at[kind + 1])
        for sem in (kind + 2, kind + 3):
            settle(buf.at[0:n - 1, 0:n // 2], send_sem.at[sem])

    settle(tiles.at[1:n], t_send)
    settle(runs.at[1:n], r_send)
    settle(rows.at[0:ny - 1, 0], y_send)
    settle(rows.at[:, core], p_send)


def solution(mesh):
    n = 1
    while n * n < mesh.shape["occ"]:
        n += 1
    ny = mesh.shape["aux"] // 2

    def per_device(ri, occ_ids, virt_ids, counts, mask, occ_energy, virt_energy, frequency):
        _, depth, cols = ri.shape
        run = cols // (n * n)
        n_rows = 2 * ny * run
        total = n * n * depth
        half = cols // 2
        aux_block = cols * 2 * ny // mask.shape[1]
        virt = virt_energy.reshape(-1, 128)
        dma = pltpu.SemaphoreType.DMA
        return pl.pallas_call(
            functools.partial(kernel, n, ny, aux_block),
            out_shape=jax.ShapeDtypeStruct((n_rows, cols), F32),
            in_specs=[pl.BlockSpec(memory_space=pltpu.HBM)] * 8,
            out_specs=pl.BlockSpec(memory_space=pltpu.VMEM),
            scratch_shapes=[
                pltpu.VMEM((n, n, depth, half), BF16),
                pltpu.VMEM((n, n, depth, half), BF16),
                pltpu.VMEM((2, total, half), BF16),
                pltpu.VMEM((2, n * depth, half), BF16),
                pltpu.VMEM((ny, 2, n, run, n * depth), BF16),
                pltpu.VMEM((2, n_rows, n * depth), BF16),
                pltpu.VMEM((cols // 128, depth, 128), BF16),
                pltpu.VMEM((n, depth, 128), BF16),
                pltpu.VMEM((n, run, n * depth), BF16),
                pltpu.VMEM((total, 128), F32),
                pltpu.SMEM(occ_ids.shape, jnp.int32),
                pltpu.SMEM(virt_ids.shape, jnp.int32),
                pltpu.SMEM(counts.shape, jnp.int32),
                pltpu.SMEM(occ_energy.shape, F32),
                pltpu.SMEM(frequency.shape, F32),
                pltpu.VMEM(mask.shape, jnp.int32),
                pltpu.VMEM(virt.shape, F32),
                pltpu.VMEM((2, n * n, 128), F32),
                pltpu.VMEM((n * n, 128), jnp.int32),
                pltpu.VMEM((n * n, 128), jnp.int32),
                pltpu.VMEM((n * n, 128), F32),
                pltpu.VMEM((128, 128), F32),
                dma((n, n)), dma((n, n)), dma((8,)), dma((9,)),
                dma, dma, dma, dma, dma((ny,)), dma, dma, dma,
            ],
            compiler_params=pltpu.CompilerParams(
                collective_id=0, has_side_effects=True, vmem_limit_bytes=48 * 1024 * 1024
            ),
            name="response",
        )(*(
            v if v is frequency else pltpu.with_memory_space_constraint(v, pltpu.HBM)
            for v in (occ_ids, virt_ids, counts, mask, occ_energy, frequency, virt, ri)
        ))

    placed = (P("occ", None, "aux"), P(), P(), P(), P(), P(), P(), P())
    return jax.shard_map(
        per_device, mesh=mesh, in_specs=placed, out_specs=P("occ", "aux"), check_vma=False
    )
```
